32 devices in a mesh: groups: 2 (over y), row: 8 (over z, x), col: 2 (over core).
Axes of the slice: x: 2, y: 2, z: 4, core: 2. Of those that a mesh axis runs over, the one named last changes fastest.
Arguments:
- tokens: bfloat16 [2048, 4096], P(('groups', 'row'), 'col'), parts along dimension 0, may hold values from -6 to 6
- cotangent: bfloat16 [2048, 4096], P(('groups', 'row'), 'col'), parts along dimension 0, may hold values from -0.5 to 0.5
- gate_weight: bfloat16 [14336, 4096], P('row', 'col'), may hold values from -0.09375 to 0.09375
- up_weight: bfloat16 [14336, 4096], P('row', 'col'), may hold values from -0.09375 to 0.09375
- down_weight: bfloat16 [14336, 4096], P('row', 'col'), may hold values from -0.046875 to 0.046875
- gate_dir: bfloat16 [14336, 4096], P('row', 'col'), may hold values from -0.09375 to 0.09375
- up_dir: bfloat16 [14336, 4096], P('row', 'col'), may hold values from -0.09375 to 0.09375
- down_dir: bfloat16 [14336, 4096], P('row', 'col'), may hold values from -0.046875 to 0.046875
Outputs:
- hvp_gate: bfloat16 [28672, 4096], P(('groups', 'row'), 'col'), parts along dimension 0
- hvp_up: bfloat16 [28672, 4096], P(('groups', 'row'), 'col'), parts along dimension 0
- hvp_down: bfloat16 [28672, 4096], P(('groups', 'row'), 'col'), parts along dimension 0
The draws below stay inside these ranges and needn't reach their ends.
There are 2 independent parts, one for each index of `groups`. The reference program is written for one: setup_inputs(seed, part) draws one part's arguments, and reference() takes and returns one part's arrays. A program takes and returns all parts, laid end to end along the dimension named above; an argument that names none is the same for every part. Nothing has to cross between parts.
All inputs are finite; a program needn't handle non-finite values.
Results may differ from the reference program's by a relative error of at most 0.0051.
Values may be sent and summed in bfloat16 or wider, within the bound.
No kernel may reach another device: no remote copies, remote signals or barrier semaphores. Data moves between devices by JAX's collectives and lax.ppermute only.
A program may use at most 320 MiB of HBM per device.

```python
import jax
import jax.numpy as jnp

D = 4096
FF = 14336
TOKENS = 1024


def shard_levels(key, extent, shards, least, largest):
    def one(dim, shards_of):
        heights = jax.random.uniform(jax.random.fold_in(jax.random.fold_in(key, 6), dim), (shards_of,), jnp.float32, least / len(shards), largest / len(shards))
        return jnp.repeat(jnp.exp(heights), extent[dim] // shards_of).reshape((-1,) + (1,) * (len(extent) - dim - 1))

    gain = one(*shards[0])
    for cut in shards[1:]:
        gain = gain * one(*cut)
    return gain


def bell_draw(own_key, shape, width, reach, shards=(), kind=jnp.bfloat16):
    factor_of = shard_levels(own_key, shape, shards, -0.22, 0.18) if shards else 1.0
    values = jax.random.normal(own_key, shape, jnp.float32) * width * factor_of
    return jnp.minimum(jnp.maximum(values, -reach), reach).astype(kind)


def setup_inputs(seed: int = 0, part: int = 0) -> dict:
    keys = jax.random.split(jax.random.key(seed), 9)
    own_keys = jax.random.split(jax.random.fold_in(keys[8], part), 9)
    return {
        "tokens": bell_draw(own_keys[0], (TOKENS, D), 1.0, 6.0, ((0, 8), (1, 2))),
        "cotangent": bell_draw(own_keys[1], (TOKENS, D), 0.08, 0.5, ((0, 8), (1, 2))),
        "gate_weight": bell_draw(keys[2], (FF, D), D ** -0.5, 0.09375, ((0, 8), (1, 2))),
        "up_weight": bell_draw(keys[3], (FF, D), D ** -0.5, 0.09375, ((0, 8), (1, 2))),
        "down_weight": bell_draw(keys[4], (FF, D), FF ** -0.5, 0.046875, ((0, 8), (1, 2))),
        "gate_dir": bell_draw(keys[5], (FF, D), D ** -0.5, 0.09375, ((0, 8), (1, 2))),
        "up_dir": bell_draw(keys[6], (FF, D), D ** -0.5, 0.09375, ((0, 8), (1, 2))),
        "down_dir": bell_draw(keys[7], (FF, D), FF ** -0.5, 0.046875, ((0, 8), (1, 2))),
    }


def second_order(gate_value, up_value, gate_tangent, up_tangent, grad_hidden, grad_tangent):
    sigmoid_gate = jax.nn.sigmoid(gate_value)
    activation = gate_value * sigmoid_gate
    first_slope = sigmoid_gate * (1.0 + gate_value * (1.0 - sigmoid_gate))
    second_slope = sigmoid_gate * (1.0 - sigmoid_gate) * (2.0 + gate_value * (1.0 - 2.0 * sigmoid_gate))
    hidden_dot = first_slope * gate_tangent * up_value + activation * up_tangent
    gate_dot = (grad_tangent * up_value + grad_hidden * up_tangent) * first_slope + grad_hidden * up_value * second_slope * gate_tangent
    up_dot = grad_tangent * activation + grad_hidden * first_slope * gate_tangent
    return gate_dot.astype(jnp.bfloat16), up_dot.astype(jnp.bfloat16), hidden_dot.astype(jnp.bfloat16)


def reference(tokens, cotangent, gate_weight, up_weight, down_weight, gate_dir, up_dir, down_dir):
    gate_value = jnp.dot(tokens, gate_weight.T, preferred_element_type=jnp.float32)
    up_value = jnp.dot(tokens, up_weight.T, preferred_element_type=jnp.float32)
    gate_tangent = jnp.dot(tokens, gate_dir.T, preferred_element_type=jnp.float32)
    up_tangent = jnp.dot(tokens, up_dir.T, preferred_element_type=jnp.float32)
    grad_hidden = jnp.dot(cotangent, down_weight.T, preferred_element_type=jnp.float32)
    grad_tangent = jnp.dot(cotangent, down_dir.T, preferred_element_type=jnp.float32)
    gate_dot, up_dot, hidden_dot = second_order(gate_value, up_value, gate_tangent, up_tangent, grad_hidden, grad_tangent)
    hvp_gate = jnp.dot(gate_dot.T, tokens, preferred_element_type=jnp.float32).astype(jnp.bfloat16)
    hvp_up = jnp.dot(up_dot.T, tokens, preferred_element_type=jnp.float32).astype(jnp.bfloat16)
    hvp_down = jnp.dot(hidden_dot.T, cotangent, preferred_element_type=jnp.float32).astype(jnp.bfloat16)
    return hvp_gate, hvp_up, hvp_down
```

```python
import jax
import jax.numpy as jnp
from jax import lax
from jax.experimental import pallas as pl
from jax.experimental.pallas import tpu as pltpu
from jax.sharding import PartitionSpec as P

F32 = jnp.float32
BF16 = jnp.bfloat16
VMEM_LIMIT = 56 * 1024 * 1024
TILE = 448
DEPTH = 3
RING = 4
PIECES = 4


def second_order(forward_sum, backward_sum, hidden_count):
    gate_value = forward_sum[:hidden_count]
    up_value = forward_sum[hidden_count : 2 * hidden_count]
    gate_tangent = forward_sum[2 * hidden_count : 3 * hidden_count]
    up_tangent = forward_sum[3 * hidden_count :]
    grad_hidden = backward_sum[:hidden_count]
    grad_tangent = backward_sum[hidden_count:]
    sigmoid_gate = jax.nn.sigmoid(gate_value)
    activation = gate_value * sigmoid_gate
    first_slope = sigmoid_gate * (1.0 + gate_value * (1.0 - sigmoid_gate))
    second_slope = (
        sigmoid_gate * (1.0 - sigmoid_gate) * (2.0 + gate_value * (1.0 - 2.0 * sigmoid_gate))
    )
    hidden_dot = first_slope * gate_tangent * up_value + activation * up_tangent
    gate_dot = (
        grad_tangent * up_value + grad_hidden * up_tangent
    ) * first_slope + grad_hidden * up_value * second_slope * gate_tangent
    up_dot = grad_tangent * activation + grad_hidden * first_slope * gate_tangent
    return jnp.concatenate((gate_dot, up_dot, hidden_dot), axis=0).astype(BF16)


def plain_shards(tokens, cotangent, gate_weight, up_weight, down_weight, gate_dir, up_dir, down_dir):
    hidden_count = gate_weight.shape[0]
    forward_stack = jnp.concatenate((gate_weight, up_weight, gate_dir, up_dir), axis=0)
    backward_stack = jnp.concatenate((down_weight, down_dir), axis=0)
    contract = (((1,), (1,)), ((), ()))
    token_rows = lax.all_gather(tokens, "row", axis=0, tiled=True)
    cot_rows = lax.all_gather(cotangent, "row", axis=0, tiled=True)
    forward_terms = lax.dot_general(forward_stack, token_rows, contract, preferred_element_type=F32)
    backward_terms = lax.dot_general(backward_stack, cot_rows, contract, preferred_element_type=F32)
    forward_sum, backward_sum = lax.psum((forward_terms, backward_terms), "col")
    results = second_order(forward_sum, backward_sum, hidden_count)
    paired = jnp.dot(results[: 2 * hidden_count], token_rows, preferred_element_type=F32)
    down_total = jnp.dot(results[2 * hidden_count :], cot_rows, preferred_element_type=F32)
    return (
        paired[:hidden_count].astype(BF16),
        paired[hidden_count:].astype(BF16),
        down_total.astype(BF16),
    )


def nt(a, b):
    return lax.dot_general(a, b, (((1,), (1,)), ((), ())), preferred_element_type=F32)


def slopes(products, extras, outs):
    gate_value, up_value, gate_tangent, up_tangent = products
    sigmoid = jax.nn.sigmoid(gate_value)
    rest = 1.0 - sigmoid
    activation = gate_value * sigmoid
    first = sigmoid * (1.0 + gate_value * rest)
    second = sigmoid * rest * (2.0 + gate_value * (1.0 - 2.0 * sigmoid))
    first_tangent = first * gate_tangent
    outs[0][...] = up_value * first
    outs[1][...] = up_tangent * first + up_value * (second * gate_tangent)
    outs[2][...] = activation
    outs[3][...] = first_tangent
    outs[4][...] = (first_tangent * up_value + activation * up_tangent).astype(BF16)


def combine(products, extras, outs):
    grad_hidden, grad_tangent = products
    outs[0][...] = (grad_tangent * extras[0][...] + grad_hidden * extras[1][...]).astype(BF16)
    outs[1][...] = (grad_tangent * extras[2][...] + grad_hidden * extras[3][...]).astype(BF16)


def products_kernel(epilogue, own, far, slots, far_slots, extras, outs, scratch):
    bufs, rows, sems = scratch
    step, steps = pl.program_id(0), pl.num_programs(0)
    tiles = [side[p] for p in range(len(own)) for side in (own, far)]
    count = len(tiles)
    piece = TILE // PIECES

    def start(at, index):
        ref, first = tiles[index]
        for i in range(PIECES):
            row = pl.multiple_of(first + at * TILE + i * piece, 16)
            pltpu.make_async_copy(
                ref.at[pl.ds(row, piece), :],
                bufs.at[index % RING, pl.ds(i * piece, piece), :],
                sems.at[index % RING],
            ).start()

    @pl.when(step == 0)
    def _():
        for index in range(DEPTH):
            start(0, index)
        for side, refs in ((0, slots), (1, far_slots)):
            at = 0
            for ref in refs:
                rows[side, at : at + ref.shape[0], :] = ref[...]
                at += ref.shape[0]

    products, total = [], None
    for index in range(count):
        ahead = index + DEPTH
        if ahead < count:
            start(step, ahead)
        else:

            @pl.when(step + 1 < steps)
            def _():
                start(step + 1, ahead - count)

        buf = bufs.at[index % RING]
        pltpu.make_async_copy(buf, buf, sems.at[index % RING]).wait()
        part = nt(buf[...], rows[index % 2])
        if index % 2 == 0:
            total = part
        else:
            products.append(total + part)
    epilogue(products, extras, outs)


def products_call(
    name, epilogue, core, own, far, slots, far_slots, extras, out_types, part=None, into=()
):
    features = own[0].shape[1]
    hidden = own[0].shape[0] // 2
    count = sum(slot.shape[0] for slot in slots)
    far_arrays = []
    for array, _ in far:
        if not any(array is other for other in far_arrays):
            far_arrays.append(array)
    places = [
        ([array is other for other in far_arrays].index(True), which * hidden)
        for array, which in far
    ]
    n_own, n_far, n_slots, n_side = len(own), len(far_arrays), len(slots), len(far_slots)
    base, tiles = (0, hidden // TILE) if part is None else part

    def kernel(core_ref, *refs):
        refs = list(refs)

        def take(n):
            taken, refs[:] = refs[:n], refs[n:]
            return taken

        own_refs, far_refs = take(n_own), take(n_far)
        slot_refs, side_refs = take(n_slots), take(n_side)
        extra_refs, _, out_refs = take(len(extras)), take(len(into)), take(len(out_types))
        products_kernel(
            epilogue,
            [(ref, core_ref[0] * hidden + base * TILE) for ref in own_refs],
            [(far_refs[i], first + base * TILE) for i, first in places],
            slot_refs,
            side_refs,
            extra_refs,
            out_refs,
            refs,
        )

    block = pl.BlockSpec((TILE, count), lambda i, c: (i + base, 0))
    whole = [pl.BlockSpec(a.shape, lambda i, c: (0, 0)) for a in (*slots, *far_slots)]
    done = tiles * TILE
    moved = 4 * len(own) * done * features + done * count * (
        4 * len(extras) + sum(jnp.dtype(t).itemsize for t in out_types)
    )
    return pl.pallas_call(
        kernel,
        out_shape=[jax.ShapeDtypeStruct((hidden, count), t) for t in out_types],
        grid_spec=pltpu.PrefetchScalarGridSpec(
            num_scalar_prefetch=1,
            grid=(tiles,),
            in_specs=[pl.BlockSpec(memory_space=pl.ANY)] * (n_own + n_far)
            + whole
            + [block] * len(extras)
            + [pl.BlockSpec(memory_space=pl.ANY)] * len(into),
            out_specs=[block] * len(out_types),
            scratch_shapes=[
                pltpu.VMEM((RING, TILE, features), BF16),
                pltpu.VMEM((2, count, features), BF16),
                pltpu.SemaphoreType.DMA((RING,)),
            ],
        ),
        compiler_params=pltpu.CompilerParams(vmem_limit_bytes=VMEM_LIMIT),
        cost_estimate=pl.CostEstimate(
            flops=4 * len(own) * done * features * count,
            bytes_accessed=moved,
            transcendentals=0,
        ),
        input_output_aliases={
            1 + n_own + n_far + n_slots + n_side + len(extras) + i: i for i in range(len(into))
        },
        name=name,
    )(core, *own, *far_arrays, *slots, *far_slots, *extras, *into)


def outer_call(name, core, products, slots):
    n_prod, n_chunks = len(products), len(products[0][0])
    half, count = products[0][0][0].shape
    features = slots[0].shape[1]
    depth = n_chunks * count
    tiles = half // TILE
    own = [chunk for pair in products for chunk in pair[0]]
    far = [chunk for pair in products for chunk in pair[1]]

    def kernel(core_ref, *refs):
        own_refs, refs = refs[: len(own)], refs[len(own) :]
        far_refs, refs = refs[: len(far)], refs[len(far) :]
        slot_refs, refs = refs[: len(slots)], refs[len(slots) :]
        outs, rows = refs[:-1], refs[-1]
        step = pl.program_id(0)

        @pl.when(step == 0)
        def _():
            at = 0
            for ref in slot_refs:
                rows[at : at + ref.shape[0], :] = ref[...]
                at += ref.shape[0]

        def work(refs):
            for prod in range(n_prod):
                chunks = refs[prod * n_chunks : (prod + 1) * n_chunks]
                left = jnp.concatenate([ref[...] for ref in chunks], axis=1)
                outs[prod][...] = jnp.dot(
                    left, rows[...], preferred_element_type=F32
                ).astype(BF16)

        pl.when(step < tiles)(lambda: work(own_refs))
        pl.when(step >= tiles)(lambda: work(far_refs))

    def place(i, c):
        return (jnp.where(i < tiles, c[0] * tiles + i, (1 - c[0]) * tiles + i - tiles), 0)

    return pl.pallas_call(
        kernel,
        out_shape=[jax.ShapeDtypeStruct((2 * half, features), BF16)] * n_prod,
        grid_spec=pltpu.PrefetchScalarGridSpec(
            num_scalar_prefetch=1,
            grid=(2 * tiles,),
            in_specs=[
                pl.BlockSpec((TILE, count), lambda i, c: (jnp.minimum(i, tiles - 1), 0))
            ] * len(own)
            + [
                pl.BlockSpec((TILE, count), lambda i, c: (jnp.maximum(i - tiles, 0), 0))
            ] * len(far)
            + [pl.BlockSpec(slot.shape, lambda i, c: (0, 0)) for slot in slots],
            out_specs=[pl.BlockSpec((TILE, features), place)] * n_prod,
            scratch_shapes=[pltpu.VMEM((depth, features), BF16)],
        ),
        compiler_params=pltpu.CompilerParams(vmem_limit_bytes=VMEM_LIMIT),
        cost_estimate=pl.CostEstimate(
            flops=4 * n_prod * half * features * depth,
            bytes_accessed=2 * (2 * n_prod * half * (features + depth) + depth * features),
            transcendentals=0,
        ),
        name=name,
    )(core, *own, *far, *slots)


def line_pairs(pairs):
    return [(2 * a + x, 2 * b + x) for a, b in pairs for x in range(2)]


X_SWAP = [(r, r ^ 1) for r in range(8)]
X_ENDS = [(r, r ^ 1) for r in (0, 1, 6, 7)]
OUTER = line_pairs([(0, 1), (1, 0), (2, 3), (3, 2)])
OUTWARD = line_pairs([(1, 0), (2, 3)])
INNER = line_pairs([(1, 2), (2, 1)])


def send(value, pairs):
    return lax.ppermute(value, "row", pairs)


def core_swap(*values):
    value = values[0] if len(values) == 1 else jnp.concatenate(values, axis=0)
    return lax.ppermute(value, "col", [(0, 1), (1, 0)])


def tie(*values):
    return lax.optimization_barrier(values)


def shards(tokens, cotangent, gate_weight, up_weight, down_weight, gate_dir, up_dir, down_dir):
    core = lax.axis_index("col")
    line = lax.axis_index("row") // 2
    inner = (line == 1) | (line == 2)
    half = gate_weight.shape[0] // 2
    here = core.reshape(1).astype(jnp.int32)

    def pick(a, b):
        return jnp.where(inner, a, b)

    def lend(*weights):
        return core_swap(
            *[lax.dynamic_slice_in_dim(w, (1 - core) * half, half, 0) for w in weights]
        )

    t0, c0 = tokens, cotangent
    ta1, tb1, tx1 = send(t0, OUTER), send(t0, INNER), send(t0, X_SWAP)
    gate_far = lend(gate_weight)
    gate_dir_far = lend(gate_dir)
    t0, ta1, tb1, tx1, gate_far, gate_dir_far, up_weight, up_dir = tie(
        t0, ta1, tb1, tx1, gate_far, gate_dir_far, up_weight, up_dir
    )
    ta2, tb2, tx2 = send(tb1, OUTWARD), send(ta1, INNER), send(ta1, X_SWAP)
    up_far = lend(up_weight)
    up_dir_far = lend(up_dir)
    ts2 = pick(tb1, ta2)
    c0, ts2, tb2, tx2, up_far, up_dir_far = tie(c0, ts2, tb2, tx2, up_far, up_dir_far)
    t_far1 = core_swap(t0, ta1, tx1, tx2)
    ta3, tx3 = send(tb2, OUTWARD), send(ts2, X_SWAP)
    ca1, cb1, cx1 = send(c0, OUTER), send(c0, INNER), send(c0, X_SWAP)

    def forward(name, slots, far_slots, part=None, into=()):
        return products_call(
            name, slopes, here,
            [gate_weight, up_weight, gate_dir, up_dir],
            [(gate_far, 0), (up_far, 0), (gate_dir_far, 0), (up_dir_far, 0)],
            slots, far_slots, [], [F32] * 4 + [BF16], part, into,
        )

    def backward(name, slots, far_slots, coefs):
        return products_call(
            name, combine, here,
            [down_weight, down_dir], [(down_far, 0), (down_dir_far, 0)],
            slots, far_slots, coefs, [BF16, BF16],
        )

    first = forward("forward1", [t0, ta1, tx1, tx2], [t_far1])
    ts3 = pick(tb2, ta3)
    ts3, tx3, ca1, cb1, cx1, first, down_weight, down_dir = tie(
        ts3, tx3, ca1, cb1, cx1, first, down_weight, down_dir
    )
    down_far, down_dir_far = lend(down_weight), lend(down_dir)
    tx4 = send(ts3, X_SWAP)
    ca2, cb2 = send(pick(cb1, cx1), OUTER), send(ca1, INNER)
    tx4, ca2, cb2, down_far, down_dir_far = tie(tx4, ca2, cb2, down_far, down_dir_far)
    t_far2 = core_swap(ts2, ts3, tx3, tx4)
    cx2, ca3, cb3 = send(pick(cb1, ca1), X_SWAP), send(cb2, OUTWARD), send(ca2, INNER)
    slots2 = [ts2, ts3, tx3, tx4]
    second = forward("forward2a", slots2, [t_far2], (0, 1))
    cx2, ca3, cb3, second, t_far2 = tie(cx2, ca3, cb3, second, t_far2)
    cs2, cs3, cs5 = pick(cb1, ca2), pick(cb2, ca3), pick(ca2, cx2)
    cx3, ca4 = send(ca2, X_ENDS), send(cb3, OUTWARD)
    *coefs1, hidden1 = first
    hidden_far1 = core_swap(hidden1)
    c_far1 = core_swap(c0, ca1, cx1, cs5)
    *coefs2, hidden2 = forward("forward2b", slots2, [t_far2], (1, half // TILE - 1), second)
    cx3, ca4, hidden_far1, c_far1, coefs2, hidden2 = tie(
        cx3, ca4, hidden_far1, c_far1, coefs2, hidden2
    )
    cs6, cs7 = pick(cx2, cx3), pick(cb3, ca4)
    c_far2 = core_swap(cs2, cs3, cs6, cs7)
    hidden_far2 = core_swap(hidden2)
    gate1, up1 = backward("backward1", [c0, ca1, cx1, cs5], [c_far1], coefs1)
    c_far2, hidden_far2, gate1, up1 = tie(c_far2, hidden_far2, gate1, up1)
    gate_far1, up_far1 = core_swap(gate1), core_swap(up1)
    gate2, up2 = backward("backward2", [cs2, cs3, cs6, cs7], [c_far2], coefs2)
    gate2, up2, gate_far1, up_far1 = tie(gate2, up2, gate_far1, up_far1)
    gate_far2, up_far2 = core_swap(gate2), core_swap(up2)
    (hvp_down,) = outer_call(
        "hvp_down", here,
        [([hidden1, hidden2], [hidden_far1, hidden_far2])],
        [c0, ca1, cx1, cs5, cs2, cs3, cs6, cs7],
    )
    hvp_down, gate_far2, up_far2 = tie(hvp_down, gate_far2, up_far2)
    hvp_gate, hvp_up = outer_call(
        "hvp_pair", here,
        [
            ([gate1, gate2], [gate_far1, gate_far2]),
            ([up1, up2], [up_far1, up_far2]),
        ],
        [t0, ta1, tx1, tx2, ts2, ts3, tx3, tx4],
    )
    return (hvp_gate, hvp_up, hvp_down)


def solution(mesh):
    in_specs = (P(("groups", "row"), "col"),) * 2 + (P("row", "col"),) * 6
    out_specs = (P(("groups", "row"), "col"),) * 3

    def run(tokens, cotangent, *weights):
        rows, cols = mesh.shape["row"], mesh.shape["col"]
        block = tokens.shape[0] // (mesh.shape["groups"] * rows)
        hidden = weights[0].shape[0] // rows
        features = tokens.shape[1] // cols
        fits = (
            rows == 8 and cols == 2 and block % 128 == 0
            and hidden % (2 * TILE) == 0 and features % 128 == 0
        )
        body = shards if fits else plain_shards
        return jax.shard_map(
            body, mesh=mesh, in_specs=in_specs, out_specs=out_specs, check_vma=False
        )(tokens, cotangent, *weights)

    return run
```

```python
import jax
import jax.numpy as jnp
from jax import lax
from jax.experimental import pallas as pl
from jax.experimental.pallas import tpu as pltpu
from jax.sharding import PartitionSpec as P

F32 = jnp.float32
BF16 = jnp.bfloat16
VMEM_LIMIT = 56 * 1024 * 1024
TILE = 448
DEPTH = 3
RING = 4
PIECES = 4


def second_order(forward_sum, backward_sum, hidden_count):
    gate_value = forward_sum[:hidden_count]
    up_value = forward_sum[hidden_count : 2 * hidden_count]
    gate_tangent = forward_sum[2 * hidden_count : 3 * hidden_count]
    up_tangent = forward_sum[3 * hidden_count :]
    grad_hidden = backward_sum[:hidden_count]
    grad_tangent = backward_sum[hidden_count:]
    sigmoid_gate = jax.nn.sigmoid(gate_value)
    activation = gate_value * sigmoid_gate
    first_slope = sigmoid_gate * (1.0 + gate_value * (1.0 - sigmoid_gate))
    second_slope = (
        sigmoid_gate * (1.0 - sigmoid_gate) * (2.0 + gate_value * (1.0 - 2.0 * sigmoid_gate))
    )
    hidden_dot = first_slope * gate_tangent * up_value + activation * up_tangent
    gate_dot = (
        grad_tangent * up_value + grad_hidden * up_tangent
    ) * first_slope + grad_hidden * up_value * second_slope * gate_tangent
    up_dot = grad_tangent * activation + grad_hidden * first_slope * gate_tangent
    return jnp.concatenate((gate_dot, up_dot, hidden_dot), axis=0).astype(BF16)


def plain_shards(tokens, cotangent, gate_weight, up_weight, down_weight, gate_dir, up_dir, down_dir):
    hidden_count = gate_weight.shape[0]
    forward_stack = jnp.concatenate((gate_weight, up_weight, gate_dir, up_dir), axis=0)
    backward_stack = jnp.concatenate((down_weight, down_dir), axis=0)
    contract = (((1,), (1,)), ((), ()))
    token_rows = lax.all_gather(tokens, "row", axis=0, tiled=True)
    cot_rows = lax.all_gather(cotangent, "row", axis=0, tiled=True)
    forward_terms = lax.dot_general(forward_stack, token_rows, contract, preferred_element_type=F32)
    backward_terms = lax.dot_general(backward_stack, cot_rows, contract, preferred_element_type=F32)
    forward_sum, backward_sum = lax.psum((forward_terms, backward_terms), "col")
    results = second_order(forward_sum, backward_sum, hidden_count)
    paired = jnp.dot(results[: 2 * hidden_count], token_rows, preferred_element_type=F32)
    down_total = jnp.dot(results[2 * hidden_count :], cot_rows, preferred_element_type=F32)
    return (
        paired[:hidden_count].astype(BF16),
        paired[hidden_count:].astype(BF16),
        down_total.astype(BF16),
    )


def nt(a, b):
    return lax.dot_general(a, b, (((1,), (1,)), ((), ())), preferred_element_type=F32)


def slopes(products, extras, outs):
    gate_value, up_value, gate_tangent, up_tangent = products
    sigmoid = jax.nn.sigmoid(gate_value)
    rest = 1.0 - sigmoid
    activation = gate_value * sigmoid
    first = sigmoid * (1.0 + gate_value * rest)
    second = sigmoid * rest * (2.0 + gate_value * (1.0 - 2.0 * sigmoid))
    first_tangent = first * gate_tangent
    outs[0][...] = up_value * first
    outs[1][...] = up_tangent * first + up_value * (second * gate_tangent)
    outs[2][...] = activation
    outs[3][...] = first_tangent
    outs[4][...] = (first_tangent * up_value + activation * up_tangent).astype(BF16)


def combine(products, extras, outs):
    grad_hidden, grad_tangent = products
    outs[0][...] = (grad_tangent * extras[0][...] + grad_hidden * extras[1][...]).astype(BF16)
    outs[1][...] = (grad_tangent * extras[2][...] + grad_hidden * extras[3][...]).astype(BF16)


def products_kernel(epilogue, own, far, rows, extras, outs, scratch):
    bufs, sems = scratch
    step, steps = pl.program_id(0), pl.num_programs(0)
    tiles = [side[p] for p in range(len(own)) for side in (own, far)]
    count = len(tiles)
    piece = TILE // PIECES

    def start(at, index):
        ref, first = tiles[index]
        for i in range(PIECES):
            row = pl.multiple_of(first + at * TILE + i * piece, 16)
            pltpu.make_async_copy(
                ref.at[pl.ds(row, piece), :],
                bufs.at[index % RING, pl.ds(i * piece, piece), :],
                sems.at[index % RING],
            ).start()

    @pl.when(step == 0)
    def _():
        for index in range(DEPTH):
            start(0, index)

    products, total = [], None
    for index in range(count):
        ahead = index + DEPTH
        if ahead < count:
            start(step, ahead)
        else:

            @pl.when(step + 1 < steps)
            def _():
                start(step + 1, ahead - count)

        buf = bufs.at[index % RING]
        pltpu.make_async_copy(buf, buf, sems.at[index % RING]).wait()
        part = nt(buf[...], rows[index % 2][...])
        if index % 2 == 0:
            total = part
        else:
            products.append(total + part)
    epilogue(products, extras, outs)


def products_call(
    name, epilogue, core, own, far, near_rows, far_rows, extras, out_types, part=None, into=()
):
    features = own[0].shape[1]
    hidden = own[0].shape[0] // 2
    count = near_rows.shape[0]
    far_arrays = []
    for array, _ in far:
        if not any(array is other for other in far_arrays):
            far_arrays.append(array)
    places = [
        ([array is other for other in far_arrays].index(True), which * hidden)
        for array, which in far
    ]
    n_own, n_far = len(own), len(far_arrays)
    base, tiles = (0, hidden // TILE) if part is None else part

    def kernel(core_ref, *refs):
        refs = list(refs)

        def take(n):
            taken, refs[:] = refs[:n], refs[n:]
            return taken

        own_refs, far_refs = take(n_own), take(n_far)
        row_refs = take(2)
        extra_refs, _, out_refs = take(len(extras)), take(len(into)), take(len(out_types))
        products_kernel(
            epilogue,
            [(ref, core_ref[0] * hidden + base * TILE) for ref in own_refs],
            [(far_refs[i], first + base * TILE) for i, first in places],
            row_refs,
            extra_refs,
            out_refs,
            refs,
        )

    block = pl.BlockSpec((TILE, count), lambda i, c: (i + base, 0))
    whole = [pl.BlockSpec((count, features), lambda i, c: (0, 0))] * 2
    done = tiles * TILE
    moved = 4 * len(own) * done * features + done * count * (
        4 * len(extras) + sum(jnp.dtype(t).itemsize for t in out_types)
    )
    return pl.pallas_call(
        kernel,
        out_shape=[jax.ShapeDtypeStruct((hidden, count), t) for t in out_types],
        grid_spec=pltpu.PrefetchScalarGridSpec(
            num_scalar_prefetch=1,
            grid=(tiles,),
            in_specs=[pl.BlockSpec(memory_space=pl.ANY)] * (n_own + n_far)
            + whole
            + [block] * len(extras)
            + [pl.BlockSpec(memory_space=pl.ANY)] * len(into),
            out_specs=[block] * len(out_types),
            scratch_shapes=[
                pltpu.VMEM((RING, TILE, features), BF16),
                pltpu.SemaphoreType.DMA((RING,)),
            ],
        ),
        compiler_params=pltpu.CompilerParams(vmem_limit_bytes=VMEM_LIMIT),
        cost_estimate=pl.CostEstimate(
            flops=4 * len(own) * done * features * count,
            bytes_accessed=moved,
            transcendentals=0,
        ),
        input_output_aliases={
            3 + n_own + n_far + len(extras) + i: i for i in range(len(into))
        },
        name=name,
    )(core, *own, *far_arrays, near_rows, far_rows, *extras, *into)


def outer_call(name, core, products, slots):
    n_prod, n_chunks = len(products), len(products[0][0])
    half, count = products[0][0][0].shape
    features = slots[0].shape[1]
    depth = n_chunks * count
    tiles = half // TILE
    own = [chunk for pair in products for chunk in pair[0]]
    far = [chunk for pair in products for chunk in pair[1]]

    def kernel(core_ref, *refs):
        own_refs, refs = refs[: len(own)], refs[len(own) :]
        far_refs, refs = refs[: len(far)], refs[len(far) :]
        slot_refs, refs = refs[: len(slots)], refs[len(slots) :]
        outs = refs
        step = pl.program_id(0)

        def work(refs):
            for prod in range(n_prod):
                chunks = refs[prod * n_chunks : (prod + 1) * n_chunks]
                total = None
                for chunk, rows in zip(chunks, slot_refs):
                    part = jnp.dot(chunk[...], rows[...], preferred_element_type=F32)
                    total = part if total is None else total + part
                outs[prod][...] = total.astype(BF16)

        pl.when(step < tiles)(lambda: work(own_refs))
        pl.when(step >= tiles)(lambda: work(far_refs))

    def place(i, c):
        return (jnp.where(i < tiles, c[0] * tiles + i, (1 - c[0]) * tiles + i - tiles), 0)

    return pl.pallas_call(
        kernel,
        out_shape=[jax.ShapeDtypeStruct((2 * half, features), BF16)] * n_prod,
        grid_spec=pltpu.PrefetchScalarGridSpec(
            num_scalar_prefetch=1,
            grid=(2 * tiles,),
            in_specs=[
                pl.BlockSpec((TILE, count), lambda i, c: (jnp.minimum(i, tiles - 1), 0))
            ] * len(own)
            + [
                pl.BlockSpec((TILE, count), lambda i, c: (jnp.maximum(i - tiles, 0), 0))
            ] * len(far)
            + [pl.BlockSpec(slot.shape, lambda i, c: (0, 0)) for slot in slots],
            out_specs=[pl.BlockSpec((TILE, features), place)] * n_prod,
        ),
        compiler_params=pltpu.CompilerParams(vmem_limit_bytes=VMEM_LIMIT),
        cost_estimate=pl.CostEstimate(
            flops=4 * n_prod * half * features * depth,
            bytes_accessed=2 * (2 * n_prod * half * (features + depth) + depth * features),
            transcendentals=0,
        ),
        name=name,
    )(core, *own, *far, *slots)


def line_pairs(pairs):
    return [(2 * a + x, 2 * b + x) for a, b in pairs for x in range(2)]


X_SWAP = [(r, r ^ 1) for r in range(8)]
OUTER = line_pairs([(0, 1), (1, 0), (2, 3), (3, 2)])
OUTWARD = line_pairs([(1, 0), (2, 3)])
INNER = line_pairs([(1, 2), (2, 1)])


def send(value, pairs):
    return lax.ppermute(value, "row", pairs)


def core_swap(value):
    return lax.ppermute(value, "col", [(0, 1), (1, 0)])


def stack(*values):
    return jnp.concatenate(values, axis=0)


def tie(*values):
    return lax.optimization_barrier(values)


def shards(tokens, cotangent, gate_weight, up_weight, down_weight, gate_dir, up_dir, down_dir):
    core = lax.axis_index("col")
    line = lax.axis_index("row") // 2
    inner = (line == 1) | (line == 2)
    half = gate_weight.shape[0] // 2
    here = core.reshape(1).astype(jnp.int32)

    def pick(a, b):
        return jnp.where(inner, a, b)

    def lent(weight):
        return lax.dynamic_slice_in_dim(weight, (1 - core) * half, half, 0)

    t0, c0 = tokens, cotangent
    ta1, tb1, tx1 = send(t0, OUTER), send(t0, INNER), send(t0, X_SWAP)
    gate_far, gate_dir_far = core_swap(lent(gate_weight)), core_swap(lent(gate_dir))
    up_lent, up_dir_lent = lent(up_weight), lent(up_dir)
    t0, ta1, tb1, tx1, gate_far, gate_dir_far, up_lent, up_dir_lent, down_weight, down_dir = tie(
        t0, ta1, tb1, tx1, gate_far, gate_dir_far, up_lent, up_dir_lent, down_weight, down_dir
    )
    ta2, tb2, tx2 = send(tb1, OUTWARD), send(ta1, INNER), send(ta1, X_SWAP)
    up_far, up_dir_far = core_swap(up_lent), core_swap(up_dir_lent)
    down_lent, down_dir_lent = lent(down_weight), lent(down_dir)
    ta2, tb2, tx2, up_far, up_dir_far, down_lent, down_dir_lent = tie(
        ta2, tb2, tx2, up_far, up_dir_far, down_lent, down_dir_lent
    )

    def forward(name, rows, far_rows, part, into=()):
        return products_call(
            name, slopes, here,
            [gate_weight, up_weight, gate_dir, up_dir],
            [(gate_far, 0), (up_far, 0), (gate_dir_far, 0), (up_dir_far, 0)],
            rows, far_rows, [], [F32] * 4 + [BF16], part, into,
        )

    def backward(name, rows, far_rows, coefs):
        return products_call(
            name, combine, here,
            [down_weight, down_dir], [(down_far, 0), (down_dir_far, 0)],
            rows, far_rows, coefs, [BF16, BF16],
        )

    lower, upper = (0, half // TILE // 2), (half // TILE // 2, half // TILE - half // TILE // 2)
    t_rows1 = stack(t0, ta1, tx1, tx2)
    t_far1 = core_swap(t_rows1)
    ts2 = pick(tb1, ta2)
    ta3, tx3 = send(tb2, OUTWARD), send(ts2, X_SWAP)
    first = forward("forward1a", t_rows1, t_far1, lower)
    ta3, tx3, ts2, c0, t_rows1, t_far1, first = tie(ta3, tx3, ts2, c0, t_rows1, t_far1, first)
    ts3 = pick(tb2, ta3)
    tx4, ca1, cb1 = send(ts3, X_SWAP), send(c0, OUTER), send(c0, INNER)
    down_far, down_dir_far = core_swap(down_lent), core_swap(down_dir_lent)
    *coefs1, hidden1 = forward("forward1b", t_rows1, t_far1, upper, first)
    tx4, ts3, c0, ca1, cb1, down_far, down_dir_far, coefs1, hidden1 = tie(
        tx4, ts3, c0, ca1, cb1, down_far, down_dir_far, coefs1, hidden1
    )
    t_rows2 = stack(ts2, ts3, tx3, tx4)
    t_far2 = core_swap(t_rows2)
    ca2, cb2, cx1 = send(cb1, OUTWARD), send(ca1, INNER), send(c0, X_SWAP)
    late, _ = tie(ca1, t_far2)
    cx2 = send(late, X_SWAP)
    second = forward("forward2a", t_rows2, t_far2, lower)
    ca2, cb2, cx1, cx2, t_rows2, t_far2, second = tie(ca2, cb2, cx1, cx2, t_rows2, t_far2, second)
    cs2 = pick(cb1, ca2)
    ca3, cx3 = send(cb2, OUTWARD), send(cs2, X_SWAP)
    c_rows1 = stack(c0, ca1, cx1, cx2)
    c_far1 = core_swap(c_rows1)
    hidden_far1 = core_swap(hidden1)
    *coefs2, hidden2 = forward("forward2b", t_rows2, t_far2, upper, second)
    ca3, cx3, c_far1, hidden_far1, coefs2, hidden2 = tie(
        ca3, cx3, c_far1, hidden_far1, coefs2, hidden2
    )
    cs3 = pick(cb2, ca3)
    cx4 = send(cs3, X_SWAP)
    hidden_far2 = core_swap(hidden2)
    gate1, up1 = backward("backward1", c_rows1, c_far1, coefs1)
    cx4, hidden_far2, gate1, up1 = tie(cx4, hidden_far2, gate1, up1)
    c_rows2 = stack(cs2, cs3, cx3, cx4)
    c_far2 = core_swap(c_rows2)
    gate_far1, up_far1 = core_swap(gate1), core_swap(up1)
    (hvp_down,) = outer_call(
        "hvp_down", here, [([hidden1, hidden2], [hidden_far1, hidden_far2])], [c_rows1, c_rows2]
    )
    hvp_down, c_far2, gate_far1, up_far1 = tie(hvp_down, c_far2, gate_far1, up_far1)
    gate2, up2 = backward("backward2", c_rows2, c_far2, coefs2)
    gate_far2, up_far2 = core_swap(gate2), core_swap(up2)
    hvp_gate, hvp_up = outer_call(
        "hvp_pair", here,
        [
            ([gate1, gate2], [gate_far1, gate_far2]),
            ([up1, up2], [up_far1, up_far2]),
        ],
        [t_rows1, t_rows2],
    )
    return (hvp_gate, hvp_up, hvp_down)


def solution(mesh):
    in_specs = (P(("groups", "row"), "col"),) * 2 + (P("row", "col"),) * 6
    out_specs = (P(("groups", "row"), "col"),) * 3

    def run(tokens, cotangent, *weights):
        rows, cols = mesh.shape["row"], mesh.shape["col"]
        block = tokens.shape[0] // (mesh.shape["groups"] * rows)
        hidden = weights[0].shape[0] // rows
        features = tokens.shape[1] // cols
        fits = (
            rows == 8 and cols == 2 and block % 128 == 0
            and hidden % (2 * TILE) == 0 and features % 128 == 0
        )
        body = shards if fits else plain_shards
        return jax.shard_map(
            body, mesh=mesh, in_specs=in_specs, out_specs=out_specs, check_vma=False
        )(tokens, cotangent, *weights)

    return run
```

```python
import jax
import jax.numpy as jnp
from jax import lax
from jax.experimental import pallas as pl
from jax.experimental.pallas import tpu as pltpu
from jax.sharding import PartitionSpec as P

F32 = jnp.float32
BF16 = jnp.bfloat16
VMEM_LIMIT = 38 * 1024 * 1024
TILE = 448
DEPTH = 3
RING = 4
PIECES = 4


def second_order(forward_sum, backward_sum, hidden_count):
    gate_value = forward_sum[:hidden_count]
    up_value = forward_sum[hidden_count : 2 * hidden_count]
    gate_tangent = forward_sum[2 * hidden_count : 3 * hidden_count]
    up_tangent = forward_sum[3 * hidden_count :]
    grad_hidden = backward_sum[:hidden_count]
    grad_tangent = backward_sum[hidden_count:]
    sigmoid_gate = jax.nn.sigmoid(gate_value)
    activation = gate_value * sigmoid_gate
    first_slope = sigmoid_gate * (1.0 + gate_value * (1.0 - sigmoid_gate))
    second_slope = (
        sigmoid_gate * (1.0 - sigmoid_gate) * (2.0 + gate_value * (1.0 - 2.0 * sigmoid_gate))
    )
    hidden_dot = first_slope * gate_tangent * up_value + activation * up_tangent
    gate_dot = (
        grad_tangent * up_value + grad_hidden * up_tangent
    ) * first_slope + grad_hidden * up_value * second_slope * gate_tangent
    up_dot = grad_tangent * activation + grad_hidden * first_slope * gate_tangent
    return jnp.concatenate((gate_dot, up_dot, hidden_dot), axis=0).astype(BF16)


def plain_shards(tokens, cotangent, gate_weight, up_weight, down_weight, gate_dir, up_dir, down_dir):
    hidden_count = gate_weight.shape[0]
    forward_stack = jnp.concatenate((gate_weight, up_weight, gate_dir, up_dir), axis=0)
    backward_stack = jnp.concatenate((down_weight, down_dir), axis=0)
    contract = (((1,), (1,)), ((), ()))
    token_rows = lax.all_gather(tokens, "row", axis=0, tiled=True)
    cot_rows = lax.all_gather(cotangent, "row", axis=0, tiled=True)
    forward_terms = lax.dot_general(forward_stack, token_rows, contract, preferred_element_type=F32)
    backward_terms = lax.dot_general(backward_stack, cot_rows, contract, preferred_element_type=F32)
    forward_sum, backward_sum = lax.psum((forward_terms, backward_terms), "col")
    results = second_order(forward_sum, backward_sum, hidden_count)
    paired = jnp.dot(results[: 2 * hidden_count], token_rows, preferred_element_type=F32)
    down_total = jnp.dot(results[2 * hidden_count :], cot_rows, preferred_element_type=F32)
    return (
        paired[:hidden_count].astype(BF16),
        paired[hidden_count:].astype(BF16),
        down_total.astype(BF16),
    )


def nt(a, b):
    return lax.dot_general(a, b, (((1,), (1,)), ((), ())), preferred_element_type=F32)


def slopes(products, extras, outs):
    gate_value, up_value, gate_tangent, up_tangent = products
    sigmoid = jax.nn.sigmoid(gate_value)
    rest = 1.0 - sigmoid
    activation = gate_value * sigmoid
    first = sigmoid * (1.0 + gate_value * rest)
    second = sigmoid * rest * (2.0 + gate_value * (1.0 - 2.0 * sigmoid))
    first_tangent = first * gate_tangent
    outs[0][...] = up_value * first
    outs[1][...] = up_tangent * first + up_value * (second * gate_tangent)
    outs[2][...] = activation
    outs[3][...] = first_tangent
    outs[4][...] = (first_tangent * up_value + activation * up_tangent).astype(BF16)


def combine(products, extras, outs):
    grad_hidden, grad_tangent = products
    outs[0][...] = (grad_tangent * extras[0][...] + grad_hidden * extras[1][...]).astype(BF16)
    outs[1][...] = (grad_tangent * extras[2][...] + grad_hidden * extras[3][...]).astype(BF16)


def products_kernel(epilogue, own, far, rows, extras, outs, scratch):
    bufs, sems = scratch
    step, steps = pl.program_id(0), pl.num_programs(0)
    tiles = [side[p] for p in range(len(own)) for side in (own, far)]
    count = len(tiles)
    piece = TILE // PIECES

    def start(at, index):
        ref, first = tiles[index]
        for i in range(PIECES):
            row = pl.multiple_of(first + at * TILE + i * piece, 16)
            pltpu.make_async_copy(
                ref.at[pl.ds(row, piece), :],
                bufs.at[index % RING, pl.ds(i * piece, piece), :],
                sems.at[index % RING],
            ).start()

    @pl.when(step == 0)
    def _():
        for index in range(DEPTH):
            start(0, index)

    products, total = [], None
    for index in range(count):
        ahead = index + DEPTH
        if ahead < count:
            start(step, ahead)
        else:

            @pl.when(step + 1 < steps)
            def _():
                start(step + 1, ahead - count)

        buf = bufs.at[index % RING]
        pltpu.make_async_copy(buf, buf, sems.at[index % RING]).wait()
        part = nt(buf[...], rows[index % 2][...])
        if index % 2 == 0:
            total = part
        else:
            products.append(total + part)
    epilogue(products, extras, outs)


def products_call(
    name, epilogue, core, own, far, near_rows, far_rows, extras, out_types, part=None, into=()
):
    features = own[0].shape[1]
    hidden = own[0].shape[0] // 2
    count = near_rows.shape[0]
    far_arrays = []
    for array, _ in far:
        if not any(array is other for other in far_arrays):
            far_arrays.append(array)
    places = [
        ([array is other for other in far_arrays].index(True), which * hidden)
        for array, which in far
    ]
    n_own, n_far = len(own), len(far_arrays)
    base, tiles = (0, hidden // TILE) if part is None else part

    def kernel(core_ref, *refs):
        refs = list(refs)

        def take(n):
            taken, refs[:] = refs[:n], refs[n:]
            return taken

        own_refs, far_refs = take(n_own), take(n_far)
        row_refs = take(2)
        extra_refs, _, out_refs = take(len(extras)), take(len(into)), take(len(out_types))
        products_kernel(
            epilogue,
            [(ref, core_ref[0] * hidden + base * TILE) for ref in own_refs],
            [(far_refs[i], first + base * TILE) for i, first in places],
            row_refs,
            extra_refs,
            out_refs,
            refs,
        )

    block = pl.BlockSpec((TILE, count), lambda i, c: (i + base, 0))
    whole = [pl.BlockSpec((count, features), lambda i, c: (0, 0))] * 2
    done = tiles * TILE
    moved = 4 * len(own) * done * features + done * count * (
        4 * len(extras) + sum(jnp.dtype(t).itemsize for t in out_types)
    )
    return pl.pallas_call(
        kernel,
        out_shape=[jax.ShapeDtypeStruct((hidden, count), t) for t in out_types],
        grid_spec=pltpu.PrefetchScalarGridSpec(
            num_scalar_prefetch=1,
            grid=(tiles,),
            in_specs=[pl.BlockSpec(memory_space=pl.ANY)] * (n_own + n_far)
            + whole
            + [block] * len(extras)
            + [pl.BlockSpec(memory_space=pl.ANY)] * len(into),
            out_specs=[block] * len(out_types),
            scratch_shapes=[
                pltpu.VMEM((RING, TILE, features), BF16),
                pltpu.SemaphoreType.DMA((RING,)),
            ],
        ),
        compiler_params=pltpu.CompilerParams(vmem_limit_bytes=VMEM_LIMIT),
        cost_estimate=pl.CostEstimate(
            flops=4 * len(own) * done * features * count,
            bytes_accessed=moved,
            transcendentals=0,
        ),
        input_output_aliases={
            3 + n_own + n_far + len(extras) + i: i for i in range(len(into))
        },
        name=name,
    )(core, *own, *far_arrays, near_rows, far_rows, *extras, *into)


def outer_call(name, core, products, slots):
    n_prod, n_chunks = len(products), len(products[0][0])
    half, count = products[0][0][0].shape
    features = slots[0].shape[1]
    depth = n_chunks * count
    tiles = half // TILE
    own = [chunk for pair in products for chunk in pair[0]]
    far = [chunk for pair in products for chunk in pair[1]]

    def kernel(core_ref, *refs):
        own_refs, refs = refs[: len(own)], refs[len(own) :]
        far_refs, refs = refs[: len(far)], refs[len(far) :]
        slot_refs, refs = refs[: len(slots)], refs[len(slots) :]
        outs = refs
        step = pl.program_id(0)

        def work(refs):
            for prod in range(n_prod):
                chunks = refs[prod * n_chunks : (prod + 1) * n_chunks]
                total = None
                for chunk, rows in zip(chunks, slot_refs):
                    part = jnp.dot(chunk[...], rows[...], preferred_element_type=F32)
                    total = part if total is None else total + part
                outs[prod][...] = total.astype(BF16)

        pl.when(step < tiles)(lambda: work(own_refs))
        pl.when(step >= tiles)(lambda: work(far_refs))

    def place(i, c):
        return (jnp.where(i < tiles, c[0] * tiles + i, (1 - c[0]) * tiles + i - tiles), 0)

    return pl.pallas_call(
        kernel,
        out_shape=[jax.ShapeDtypeStruct((2 * half, features), BF16)] * n_prod,
        grid_spec=pltpu.PrefetchScalarGridSpec(
            num_scalar_prefetch=1,
            grid=(2 * tiles,),
            in_specs=[
                pl.BlockSpec((TILE, count), lambda i, c: (jnp.minimum(i, tiles - 1), 0))
            ] * len(own)
            + [
                pl.BlockSpec((TILE, count), lambda i, c: (jnp.maximum(i - tiles, 0), 0))
            ] * len(far)
            + [pl.BlockSpec(slot.shape, lambda i, c: (0, 0)) for slot in slots],
            out_specs=[pl.BlockSpec((TILE, features), place)] * n_prod,
        ),
        compiler_params=pltpu.CompilerParams(vmem_limit_bytes=VMEM_LIMIT),
        cost_estimate=pl.CostEstimate(
            flops=4 * n_prod * half * features * depth,
            bytes_accessed=2 * (2 * n_prod * half * (features + depth) + depth * features),
            transcendentals=0,
        ),
        name=name,
    )(core, *own, *far, *slots)


def line_pairs(pairs):
    return [(2 * a + x, 2 * b + x) for a, b in pairs for x in range(2)]


X_SWAP = [(r, r ^ 1) for r in range(8)]
OUTER = line_pairs([(0, 1), (1, 0), (2, 3), (3, 2)])
OUTWARD = line_pairs([(1, 0), (2, 3)])
INNER = line_pairs([(1, 2), (2, 1)])


def send(value, pairs):
    return lax.ppermute(value, "row", pairs)


def core_swap(value):
    return lax.ppermute(value, "col", [(0, 1), (1, 0)])


def stack(*values):
    return jnp.concatenate(values, axis=0)


def tie(*values):
    return lax.optimization_barrier(values)


def shards(tokens, cotangent, gate_weight, up_weight, down_weight, gate_dir, up_dir, down_dir):
    core = lax.axis_index("col")
    line = lax.axis_index("row") // 2
    inner = (line == 1) | (line == 2)
    half = gate_weight.shape[0] // 2
    here = core.reshape(1).astype(jnp.int32)

    def pick(a, b):
        return jnp.where(inner, a, b)

    def lent(weight):
        return lax.dynamic_slice_in_dim(weight, (1 - core) * half, half, 0)

    t0, c0 = tokens, cotangent
    ta1, tb1, tx1 = send(t0, OUTER), send(t0, INNER), send(t0, X_SWAP)
    gate_far, gate_dir_far = core_swap(lent(gate_weight)), core_swap(lent(gate_dir))
    up_lent, up_dir_lent = lent(up_weight), lent(up_dir)
    t0, ta1, tb1, tx1, gate_far, gate_dir_far, up_lent, up_dir_lent, down_weight, down_dir = tie(
        t0, ta1, tb1, tx1, gate_far, gate_dir_far, up_lent, up_dir_lent, down_weight, down_dir
    )
    ta2, tb2, tx2 = send(tb1, OUTWARD), send(ta1, INNER), send(ta1, X_SWAP)
    up_far, up_dir_far = core_swap(up_lent), core_swap(up_dir_lent)
    down_lent, down_dir_lent = lent(down_weight), lent(down_dir)
    ta2, tb2, tx2, up_far, up_dir_far, down_lent, down_dir_lent = tie(
        ta2, tb2, tx2, up_far, up_dir_far, down_lent, down_dir_lent
    )

    def forward(name, rows, far_rows, part, into=()):
        return products_call(
            name, slopes, here,
            [gate_weight, up_weight, gate_dir, up_dir],
            [(gate_far, 0), (up_far, 0), (gate_dir_far, 0), (up_dir_far, 0)],
            rows, far_rows, [], [F32] * 4 + [BF16], part, into,
        )

    def backward(name, rows, far_rows, coefs):
        return products_call(
            name, combine, here,
            [down_weight, down_dir], [(down_far, 0), (down_dir_far, 0)],
            rows, far_rows, coefs, [BF16, BF16],
        )

    lower, upper = (0, half // TILE // 2), (half // TILE // 2, half // TILE - half // TILE // 2)
    t_rows1 = stack(t0, ta1, tx1, tx2)
    t_far1 = core_swap(t_rows1)
    ts2 = pick(tb1, ta2)
    ta3, tx3 = send(tb2, OUTWARD), send(ts2, X_SWAP)
    first = forward("forward1a", t_rows1, t_far1, lower)
    ta3, tx3, ts2, c0, t_rows1, t_far1, first = tie(ta3, tx3, ts2, c0, t_rows1, t_far1, first)
    ts3 = pick(tb2, ta3)
    tx4, ca1, cb1 = send(ts3, X_SWAP), send(c0, OUTER), send(c0, INNER)
    down_far, down_dir_far = core_swap(down_lent), core_swap(down_dir_lent)
    *coefs1, hidden1 = forward("forward1b", t_rows1, t_far1, upper, first)
    tx4, ts3, c0, ca1, cb1, down_far, down_dir_far, coefs1, hidden1 = tie(
        tx4, ts3, c0, ca1, cb1, down_far, down_dir_far, coefs1, hidden1
    )
    t_rows2 = stack(ts2, ts3, tx3, tx4)
    t_far2 = core_swap(t_rows2)
    ca2, cb2, cx1 = send(cb1, OUTWARD), send(ca1, INNER), send(c0, X_SWAP)
    late, _ = tie(ca1, t_far2)
    cx2 = send(late, X_SWAP)
    second = forward("forward2a", t_rows2, t_far2, lower)
    ca2, cb2, cx1, cx2, t_rows2, t_far2, second = tie(ca2, cb2, cx1, cx2, t_rows2, t_far2, second)
    cs2 = pick(cb1, ca2)
    ca3, cx3 = send(cb2, OUTWARD), send(cs2, X_SWAP)
    c_rows1 = stack(c0, ca1, cx1, cx2)
    c_far1 = core_swap(c_rows1)
    hidden_far1 = core_swap(hidden1)
    *coefs2, hidden2 = forward("forward2b", t_rows2, t_far2, upper, second)
    ca3, cx3, c_far1, hidden_far1, coefs2, hidden2 = tie(
        ca3, cx3, c_far1, hidden_far1, coefs2, hidden2
    )
    cs3 = pick(cb2, ca3)
    cx4 = send(cs3, X_SWAP)
    hidden_far2 = core_swap(hidden2)
    gate1, up1 = backward("backward1", c_rows1, c_far1, coefs1)
    cx4, hidden_far2, gate1, up1 = tie(cx4, hidden_far2, gate1, up1)
    c_rows2 = stack(cs2, cs3, cx3, cx4)
    c_far2 = core_swap(c_rows2)
    gate_far1, up_far1 = core_swap(gate1), core_swap(up1)
    (hvp_down,) = outer_call(
        "hvp_down", here, [([hidden1, hidden2], [hidden_far1, hidden_far2])], [c_rows1, c_rows2]
    )
    hvp_down, c_far2, gate_far1, up_far1 = tie(hvp_down, c_far2, gate_far1, up_far1)
    gate2, up2 = backward("backward2", c_rows2, c_far2, coefs2)
    gate_far2, up_far2 = core_swap(gate2), core_swap(up2)
    hvp_gate, hvp_up = outer_call(
        "hvp_pair", here,
        [
            ([gate1, gate2], [gate_far1, gate_far2]),
            ([up1, up2], [up_far1, up_far2]),
        ],
        [t_rows1, t_rows2],
    )
    return (hvp_gate, hvp_up, hvp_down)


def solution(mesh):
    in_specs = (P(("groups", "row"), "col"),) * 2 + (P("row", "col"),) * 6
    out_specs = (P(("groups", "row"), "col"),) * 3

    def run(tokens, cotangent, *weights):
        rows, cols = mesh.shape["row"], mesh.shape["col"]
        block = tokens.shape[0] // (mesh.shape["groups"] * rows)
        hidden = weights[0].shape[0] // rows
        features = tokens.shape[1] // cols
        fits = (
            rows == 8 and cols == 2 and block % 128 == 0
            and hidden % (2 * TILE) == 0 and features % 128 == 0
        )
        body = shards if fits else plain_shards
        return jax.shard_map(
            body, mesh=mesh, in_specs=in_specs, out_specs=out_specs, check_vma=False
        )(tokens, cotangent, *weights)

    return run
```

```python
import jax
import jax.numpy as jnp
from jax import lax
from jax.experimental import pallas as pl
from jax.experimental.pallas import tpu as pltpu
from jax.sharding import PartitionSpec as P

F32 = jnp.float32
BF16 = jnp.bfloat16
VMEM_LIMIT = 33 * 1024 * 1024
TILE = 448
DEPTH = 3
RING = 4
PIECES = 4


def second_order(forward_sum, backward_sum, hidden_count):
    gate_value = forward_sum[:hidden_count]
    up_value = forward_sum[hidden_count : 2 * hidden_count]
    gate_tangent = forward_sum[2 * hidden_count : 3 * hidden_count]
    up_tangent = forward_sum[3 * hidden_count :]
    grad_hidden = backward_sum[:hidden_count]
    grad_tangent = backward_sum[hidden_count:]
    sigmoid_gate = jax.nn.sigmoid(gate_value)
    activation = gate_value * sigmoid_gate
    first_slope = sigmoid_gate * (1.0 + gate_value * (1.0 - sigmoid_gate))
    second_slope = (
        sigmoid_gate * (1.0 - sigmoid_gate) * (2.0 + gate_value * (1.0 - 2.0 * sigmoid_gate))
    )
    hidden_dot = first_slope * gate_tangent * up_value + activation * up_tangent
    gate_dot = (
        grad_tangent * up_value + grad_hidden * up_tangent
    ) * first_slope + grad_hidden * up_value * second_slope * gate_tangent
    up_dot = grad_tangent * activation + grad_hidden * first_slope * gate_tangent
    return jnp.concatenate((gate_dot, up_dot, hidden_dot), axis=0).astype(BF16)


def plain_shards(tokens, cotangent, gate_weight, up_weight, down_weight, gate_dir, up_dir, down_dir):
    hidden_count = gate_weight.shape[0]
    forward_stack = jnp.concatenate((gate_weight, up_weight, gate_dir, up_dir), axis=0)
    backward_stack = jnp.concatenate((down_weight, down_dir), axis=0)
    contract = (((1,), (1,)), ((), ()))
    token_rows = lax.all_gather(tokens, "row", axis=0, tiled=True)
    cot_rows = lax.all_gather(cotangent, "row", axis=0, tiled=True)
    forward_terms = lax.dot_general(forward_stack, token_rows, contract, preferred_element_type=F32)
    backward_terms = lax.dot_general(backward_stack, cot_rows, contract, preferred_element_type=F32)
    forward_sum, backward_sum = lax.psum((forward_terms, backward_terms), "col")
    results = second_order(forward_sum, backward_sum, hidden_count)
    paired = jnp.dot(results[: 2 * hidden_count], token_rows, preferred_element_type=F32)
    down_total = jnp.dot(results[2 * hidden_count :], cot_rows, preferred_element_type=F32)
    return (
        paired[:hidden_count].astype(BF16),
        paired[hidden_count:].astype(BF16),
        down_total.astype(BF16),
    )


def nt(a, b):
    return lax.dot_general(a, b, (((1,), (1,)), ((), ())), preferred_element_type=F32)


def slopes(products, extras, outs):
    gate_value, up_value, gate_tangent, up_tangent = products
    sigmoid = jax.nn.sigmoid(gate_value)
    rest = 1.0 - sigmoid
    activation = gate_value * sigmoid
    first = sigmoid * (1.0 + gate_value * rest)
    second = sigmoid * rest * (2.0 + gate_value * (1.0 - 2.0 * sigmoid))
    first_tangent = first * gate_tangent
    outs[0][...] = up_value * first
    outs[1][...] = up_tangent * first + up_value * (second * gate_tangent)
    outs[2][...] = activation
    outs[3][...] = first_tangent
    outs[4][...] = (first_tangent * up_value + activation * up_tangent).astype(BF16)


def combine(products, extras, outs):
    grad_hidden, grad_tangent = products
    outs[0][...] = (grad_tangent * extras[0][...] + grad_hidden * extras[1][...]).astype(BF16)
    outs[1][...] = (grad_tangent * extras[2][...] + grad_hidden * extras[3][...]).astype(BF16)


def products_kernel(epilogue, own, far, rows, extras, outs, scratch):
    bufs, sems = scratch
    step, steps = pl.program_id(0), pl.num_programs(0)
    tiles = [side[p] for p in range(len(own)) for side in (own, far)]
    count = len(tiles)
    piece = TILE // PIECES

    def start(at, index):
        ref, first = tiles[index]
        for i in range(PIECES):
            row = pl.multiple_of(first + at * TILE + i * piece, 16)
            pltpu.make_async_copy(
                ref.at[pl.ds(row, piece), :],
                bufs.at[index % RING, pl.ds(i * piece, piece), :],
                sems.at[index % RING],
            ).start()

    @pl.when(step == 0)
    def _():
        for index in range(DEPTH):
            start(0, index)

    products, total = [], None
    for index in range(count):
        ahead = index + DEPTH
        if ahead < count:
            start(step, ahead)
        else:

            @pl.when(step + 1 < steps)
            def _():
                start(step + 1, ahead - count)

        buf = bufs.at[index % RING]
        pltpu.make_async_copy(buf, buf, sems.at[index % RING]).wait()
        part = nt(buf[...], rows[index % 2][...])
        if index % 2 == 0:
            total = part
        else:
            products.append(total + part)
    epilogue(products, extras, outs)


def products_call(
    name, epilogue, core, own, far, near_rows, far_rows, extras, out_types, part=None, into=()
):
    features = own[0].shape[1]
    hidden = own[0].shape[0] // 2
    count = near_rows.shape[0]
    far_arrays = []
    for array, _ in far:
        if not any(array is other for other in far_arrays):
            far_arrays.append(array)
    places = [
        ([array is other for other in far_arrays].index(True), which * hidden)
        for array, which in far
    ]
    n_own, n_far = len(own), len(far_arrays)
    base, tiles = (0, hidden // TILE) if part is None else part

    def kernel(core_ref, *refs):
        refs = list(refs)

        def take(n):
            taken, refs[:] = refs[:n], refs[n:]
            return taken

        own_refs, far_refs = take(n_own), take(n_far)
        row_refs = take(2)
        extra_refs, _, out_refs = take(len(extras)), take(len(into)), take(len(out_types))
        products_kernel(
            epilogue,
            [(ref, core_ref[0] * hidden + base * TILE) for ref in own_refs],
            [(far_refs[i], first + base * TILE) for i, first in places],
            row_refs,
            extra_refs,
            out_refs,
            refs,
        )

    block = pl.BlockSpec((TILE, count), lambda i, c: (i + base, 0))
    whole = [pl.BlockSpec((count, features), lambda i, c: (0, 0))] * 2
    done = tiles * TILE
    moved = 4 * len(own) * done * features + done * count * (
        4 * len(extras) + sum(jnp.dtype(t).itemsize for t in out_types)
    )
    return pl.pallas_call(
        kernel,
        out_shape=[jax.ShapeDtypeStruct((hidden, count), t) for t in out_types],
        grid_spec=pltpu.PrefetchScalarGridSpec(
            num_scalar_prefetch=1,
            grid=(tiles,),
            in_specs=[pl.BlockSpec(memory_space=pl.ANY)] * (n_own + n_far)
            + whole
            + [block] * len(extras)
            + [pl.BlockSpec(memory_space=pl.ANY)] * len(into),
            out_specs=[block] * len(out_types),
            scratch_shapes=[
                pltpu.VMEM((RING, TILE, features), BF16),
                pltpu.SemaphoreType.DMA((RING,)),
            ],
        ),
        compiler_params=pltpu.CompilerParams(vmem_limit_bytes=VMEM_LIMIT),
        cost_estimate=pl.CostEstimate(
            flops=4 * len(own) * done * features * count,
            bytes_accessed=moved,
            transcendentals=0,
        ),
        input_output_aliases={
            3 + n_own + n_far + len(extras) + i: i for i in range(len(into))
        },
        name=name,
    )(core, *own, *far_arrays, near_rows, far_rows, *extras, *into)


def outer_call(name, core, products, slots):
    n_prod, n_chunks = len(products), len(products[0][0])
    half, count = products[0][0][0].shape
    features = slots[0].shape[1]
    depth = n_chunks * count
    tiles = half // TILE
    own = [chunk for pair in products for chunk in pair[0]]
    far = [chunk for pair in products for chunk in pair[1]]

    def kernel(core_ref, *refs):
        own_refs, refs = refs[: len(own)], refs[len(own) :]
        far_refs, refs = refs[: len(far)], refs[len(far) :]
        slot_refs, refs = refs[: len(slots)], refs[len(slots) :]
        outs = refs
        step = pl.program_id(0)

        def work(refs):
            for prod in range(n_prod):
                chunks = refs[prod * n_chunks : (prod + 1) * n_chunks]
                total = None
                for chunk, rows in zip(chunks, slot_refs):
                    part = jnp.dot(chunk[...], rows[...], preferred_element_type=F32)
                    total = part if total is None else total + part
                outs[prod][...] = total.astype(BF16)

        pl.when(step < tiles)(lambda: work(own_refs))
        pl.when(step >= tiles)(lambda: work(far_refs))

    def place(i, c):
        return (jnp.where(i < tiles, c[0] * tiles + i, (1 - c[0]) * tiles + i - tiles), 0)

    return pl.pallas_call(
        kernel,
        out_shape=[jax.ShapeDtypeStruct((2 * half, features), BF16)] * n_prod,
        grid_spec=pltpu.PrefetchScalarGridSpec(
            num_scalar_prefetch=1,
            grid=(2 * tiles,),
            in_specs=[
                pl.BlockSpec((TILE, count), lambda i, c: (jnp.minimum(i, tiles - 1), 0))
            ] * len(own)
            + [
                pl.BlockSpec((TILE, count), lambda i, c: (jnp.maximum(i - tiles, 0), 0))
            ] * len(far)
            + [pl.BlockSpec(slot.shape, lambda i, c: (0, 0)) for slot in slots],
            out_specs=[pl.BlockSpec((TILE, features), place)] * n_prod,
        ),
        compiler_params=pltpu.CompilerParams(vmem_limit_bytes=VMEM_LIMIT),
        cost_estimate=pl.CostEstimate(
            flops=4 * n_prod * half * features * depth,
            bytes_accessed=2 * (2 * n_prod * half * (features + depth) + depth * features),
            transcendentals=0,
        ),
        name=name,
    )(core, *own, *far, *slots)


def line_pairs(pairs):
    return [(2 * a + x, 2 * b + x) for a, b in pairs for x in range(2)]


X_SWAP = [(r, r ^ 1) for r in range(8)]
OUTER = line_pairs([(0, 1), (1, 0), (2, 3), (3, 2)])
OUTWARD = line_pairs([(1, 0), (2, 3)])
INNER = line_pairs([(1, 2), (2, 1)])


def send(value, pairs):
    return lax.ppermute(value, "row", pairs)


def core_swap(value):
    return lax.ppermute(value, "col", [(0, 1), (1, 0)])


def stack(*values):
    return jnp.concatenate(values, axis=0)


def tie(*values):
    return lax.optimization_barrier(values)


def shards(tokens, cotangent, gate_weight, up_weight, down_weight, gate_dir, up_dir, down_dir):
    core = lax.axis_index("col")
    line = lax.axis_index("row") // 2
    inner = (line == 1) | (line == 2)
    half = gate_weight.shape[0] // 2
    here = core.reshape(1).astype(jnp.int32)

    def pick(a, b):
        return jnp.where(inner, a, b)

    def lent(weight):
        return lax.dynamic_slice_in_dim(weight, (1 - core) * half, half, 0)

    t0, c0 = tokens, cotangent
    ta1, tb1, tx1 = send(t0, OUTER), send(t0, INNER), send(t0, X_SWAP)
    gate_far, gate_dir_far = core_swap(lent(gate_weight)), core_swap(lent(gate_dir))
    up_lent, up_dir_lent = lent(up_weight), lent(up_dir)
    t0, ta1, tb1, tx1, gate_far, gate_dir_far, up_lent, up_dir_lent, down_weight, down_dir = tie(
        t0, ta1, tb1, tx1, gate_far, gate_dir_far, up_lent, up_dir_lent, down_weight, down_dir
    )
    ta2, tb2, tx2 = send(tb1, OUTWARD), send(ta1, INNER), send(ta1, X_SWAP)
    up_far, up_dir_far = core_swap(up_lent), core_swap(up_dir_lent)
    down_lent, down_dir_lent = lent(down_weight), lent(down_dir)
    ta2, tb2, tx2, up_far, up_dir_far, down_lent, down_dir_lent = tie(
        ta2, tb2, tx2, up_far, up_dir_far, down_lent, down_dir_lent
    )

    def forward(name, rows, far_rows, part, into=()):
        return products_call(
            name, slopes, here,
            [gate_weight, up_weight, gate_dir, up_dir],
            [(gate_far, 0), (up_far, 0), (gate_dir_far, 0), (up_dir_far, 0)],
            rows, far_rows, [], [F32] * 4 + [BF16], part, into,
        )

    def backward(name, rows, far_rows, coefs):
        return products_call(
            name, combine, here,
            [down_weight, down_dir], [(down_far, 0), (down_dir_far, 0)],
            rows, far_rows, coefs, [BF16, BF16],
        )

    lower, upper = (0, half // TILE // 2), (half // TILE // 2, half // TILE - half // TILE // 2)
    t_rows1 = stack(t0, ta1, tx1, tx2)
    t_far1 = core_swap(t_rows1)
    ts2 = pick(tb1, ta2)
    ta3, tx3 = send(tb2, OUTWARD), send(ts2, X_SWAP)
    first = forward("forward1a", t_rows1, t_far1, lower)
    ta3, tx3, ts2, c0, t_rows1, t_far1, first = tie(ta3, tx3, ts2, c0, t_rows1, t_far1, first)
    ts3 = pick(tb2, ta3)
    tx4, ca1, cb1 = send(ts3, X_SWAP), send(c0, OUTER), send(c0, INNER)
    down_far, down_dir_far = core_swap(down_lent), core_swap(down_dir_lent)
    *coefs1, hidden1 = forward("forward1b", t_rows1, t_far1, upper, first)
    tx4, ts3, c0, ca1, cb1, down_far, down_dir_far, coefs1, hidden1 = tie(
        tx4, ts3, c0, ca1, cb1, down_far, down_dir_far, coefs1, hidden1
    )
    t_rows2 = stack(ts2, ts3, tx3, tx4)
    t_far2 = core_swap(t_rows2)
    ca2, cb2, cx1 = send(cb1, OUTWARD), send(ca1, INNER), send(c0, X_SWAP)
    late, _ = tie(ca1, t_far2)
    cx2 = send(late, X_SWAP)
    second = forward("forward2a", t_rows2, t_far2, lower)
    ca2, cb2, cx1, cx2, t_rows2, t_far2, second = tie(ca2, cb2, cx1, cx2, t_rows2, t_far2, second)
    cs2 = pick(cb1, ca2)
    ca3, cx3 = send(cb2, OUTWARD), send(cs2, X_SWAP)
    c_rows1 = stack(c0, ca1, cx1, cx2)
    c_far1 = core_swap(c_rows1)
    hidden_far1 = core_swap(hidden1)
    *coefs2, hidden2 = forward("forward2b", t_rows2, t_far2, upper, second)
    ca3, cx3, c_far1, hidden_far1, coefs2, hidden2 = tie(
        ca3, cx3, c_far1, hidden_far1, coefs2, hidden2
    )
    cs3 = pick(cb2, ca3)
    cx4 = send(cs3, X_SWAP)
    hidden_far2 = core_swap(hidden2)
    gate1, up1 = backward("backward1", c_rows1, c_far1, coefs1)
    cx4, hidden_far2, gate1, up1 = tie(cx4, hidden_far2, gate1, up1)
    c_rows2 = stack(cs2, cs3, cx3, cx4)
    c_far2 = core_swap(c_rows2)
    gate_far1, up_far1 = core_swap(gate1), core_swap(up1)
    (hvp_down,) = outer_call(
        "hvp_down", here, [([hidden1, hidden2], [hidden_far1, hidden_far2])], [c_rows1, c_rows2]
    )
    hvp_down, c_far2, gate_far1, up_far1 = tie(hvp_down, c_far2, gate_far1, up_far1)
    gate2, up2 = backward("backward2", c_rows2, c_far2, coefs2)
    gate_far2, up_far2 = core_swap(gate2), core_swap(up2)
    hvp_gate, hvp_up = outer_call(
        "hvp_pair", here,
        [
            ([gate1, gate2], [gate_far1, gate_far2]),
            ([up1, up2], [up_far1, up_far2]),
        ],
        [t_rows1, t_rows2],
    )
    return (hvp_gate, hvp_up, hvp_down)


def solution(mesh):
    in_specs = (P(("groups", "row"), "col"),) * 2 + (P("row", "col"),) * 6
    out_specs = (P(("groups", "row"), "col"),) * 3

    def run(tokens, cotangent, *weights):
        rows, cols = mesh.shape["row"], mesh.shape["col"]
        block = tokens.shape[0] // (mesh.shape["groups"] * rows)
        hidden = weights[0].shape[0] // rows
        features = tokens.shape[1] // cols
        fits = (
            rows == 8 and cols == 2 and block % 128 == 0
            and hidden % (2 * TILE) == 0 and features % 128 == 0
        )
        body = shards if fits else plain_shards
        return jax.shard_map(
            body, mesh=mesh, in_specs=in_specs, out_specs=out_specs, check_vma=False
        )(tokens, cotangent, *weights)

    return run
```
